32 devices in a mesh: grp: 2 (over y), ew: 4 (over z), ns: 2 (over x), lvl: 2 (over core).
Axes of the slice: x: 2, y: 2, z: 4, core: 2. Of those that a mesh axis runs over, the one named last changes fastest.
Arguments:
- probe_fine: int32 [8, 128, 512], P('lvl', 'ew', 'ns'), may hold values from 0 to 1
- probe_coarse: int32 [8, 64, 256], P('lvl', 'ew', 'ns'), may hold values from 0 to 1
- kappa_fine: float32 [256, 512], P(('grp', 'ew'), 'ns'), parts along dimension 0, may hold values from 0.2 to 2
- kappa_coarse: float32 [128, 256], P(('grp', 'ew'), 'ns'), parts along dimension 0, may hold values from 0.2 to 2
- phi_tiles: float32 [1024, 128, 128], P(('ew', 'ns')), may hold values from -0.5 to 0.5
- obs_weight: float32 [2048, 128], P(('grp', 'ew', 'ns')), parts along dimension 0, may hold values from 4 to 40
- block_index: int32 [1024], P(('ew', 'ns')), may hold values from 0 to 85, as said below
- block_count: int32 [8], P(('ew', 'ns')), may hold values from 2 to 128, as said below
Outputs:
- solve_fine: float32 [16, 128, 512], P(('grp', 'lvl'), 'ew', 'ns'), parts along dimension 0
- solve_coarse: float32 [16, 64, 256], P(('grp', 'lvl'), 'ew', 'ns'), parts along dimension 0
- resid_fine: float32 [16, 128, 512], P(('grp', 'lvl'), 'ew', 'ns'), parts along dimension 0
- resid_coarse: float32 [16, 64, 256], P(('grp', 'lvl'), 'ew', 'ns'), parts along dimension 0
The draws below stay inside these ranges and needn't reach their ends.
There are 2 independent parts, one for each index of `grp`. The reference program is written for one: setup_inputs(seed, part) draws one part's arguments, and reference() takes and returns one part's arrays. A program takes and returns all parts, laid end to end along the dimension named above; an argument that names none is the same for every part. Nothing has to cross between parts.
Inputs may be any that keep to these rules, and one draw needn't show every extreme that they name: `block_count`: every device has 2 or more live blocks, and only blocks below its count carry observations; some device has all 128 slots live. `block_index`: A block's tile is one of its own device's 86 tiles, in the order of the tile list; each device's first block names a tile of its western outside row (fine or coarse) and its second block a tile of its eastern outside row.
All inputs are finite; a program needn't handle non-finite values.
Results may differ from the reference program's by a relative error of at most 0.0003.
Values sent between devices are 32-bit elements; how exact they have to be, the bound alone decides.
A program may use at most 64 MiB of HBM per device.

```python
import math
import jax
import jax.numpy as jnp
from jax import lax

CX = 32
CY = 256
TILE = 128
NB = 128
ITERS = 2
P_SIZE = 8
NX = 128
NY = 512
NTE = 86
NBT = 1024
N_EW = 4
N_NS = 2


def draw_block_index(key, part):
    devices = NBT // NB
    per_row = CY // TILE
    coarse_first = (CX + 2) * per_row
    key_base, key_west, key_east = jax.random.split(jax.random.fold_in(key, 11), 3)
    chosen = jax.random.randint(key_base, (devices, NB), 0, NTE)
    pick_west = jax.random.randint(key_west, (devices,), 0, per_row + 1)
    west = jnp.where(pick_west == per_row, coarse_first, pick_west)
    pick_east = jax.random.randint(key_east, (devices,), 0, per_row + 1)
    east = jnp.where(pick_east == per_row, NTE - 1, (CX + 1) * per_row + pick_east)
    chosen = chosen.at[:, 0].set(west).at[:, 1].set(east)
    return chosen.reshape(NBT).astype(jnp.int32)


def draw_block_count(key, part):
    devices = NBT // NB
    key_counts, key_busy = jax.random.split(jax.random.fold_in(key, 23), 2)
    counts = jax.random.randint(key_counts, (devices,), 2, NB * 3 // 4 + 1)
    busiest = jax.random.randint(key_busy, (), 0, devices)
    counts = jnp.where(jnp.arange(devices, dtype=jnp.int32) == busiest, NB, counts)
    return counts.astype(jnp.int32)


def plant(drawn, own_key, least, top_value):
    extent = drawn.shape
    place = [jax.random.randint(jax.random.fold_in(own_key, axis), (), 0, extent[axis]) for axis in range(len(extent))]
    drawn = drawn.at[tuple(place)].set(least)
    longest = extent.index(max(extent))
    place[longest] = (place[longest] + 1) % extent[longest]
    return drawn.at[tuple(place)].set(top_value)


def level_of(own_key, shape, cuts, least, top_value):
    factor_of, own = 1.0, jax.random.fold_in(own_key, 6)
    for position, blocks in cuts:
        steps = jnp.exp(jax.random.uniform(jax.random.fold_in(own, position), (blocks,), jnp.float32, least / len(cuts), top_value / len(cuts)))
        factor_of = factor_of * jnp.repeat(steps, shape[position] // blocks).reshape([-1 if axis == position else 1 for axis in range(len(shape))])
    return factor_of


def centred(key, extent, width, most, cuts=(), kind=jnp.bfloat16):
    gain = level_of(key, extent, cuts, -0.22, 0.18) if cuts else 1.0
    drawn = jax.random.normal(key, extent, jnp.float32) * width * gain
    return jnp.minimum(jnp.maximum(drawn, -most), most).astype(kind)


def setup_inputs(seed: int = 0, part: int = 0) -> dict:
    arg_keys = jax.random.split(jax.random.key(seed), 9)
    own_keys = jax.random.split(jax.random.fold_in(arg_keys[8], part), 9)
    probe_fine = plant(jax.random.randint(arg_keys[0], (P_SIZE, NX, NY), 0, 2), jax.random.fold_in(arg_keys[0], 1), 0, 1).astype(jnp.int32)
    probe_coarse = plant(jax.random.randint(arg_keys[1], (P_SIZE, NX // 2, NY // 2), 0, 2), jax.random.fold_in(arg_keys[1], 1), 0, 1).astype(jnp.int32)
    kappa_fine = jnp.clip(jnp.exp(math.log(2.0) - 2.3025851 * jax.random.uniform(own_keys[2], (NX, NY), jnp.float32) ** level_of(own_keys[2], (NX, NY), ((0, 4), (1, 2)), -0.2, 0.2)), 0.2, 2.0)
    kappa_coarse = jnp.clip(jnp.exp(math.log(2.0) - 2.3025851 * jax.random.uniform(own_keys[3], (NX // 2, NY // 2), jnp.float32) ** level_of(own_keys[3], (NX // 2, NY // 2), ((0, 4), (1, 2)), -0.2, 0.2)), 0.2, 2.0)
    phi_tiles = centred(arg_keys[4], (NBT, TILE, TILE), TILE ** -0.5, 0.5, ((0, 8),), jnp.float32)
    obs_weight = jnp.clip(jnp.exp(math.log(40.0) - 2.3025851 * jax.random.uniform(own_keys[5], (NBT, TILE), jnp.float32) ** level_of(own_keys[5], (NBT, TILE), ((0, 8),), -0.2, 0.2)), 4.0, 40.0)
    block_index = draw_block_index(jax.random.fold_in(arg_keys[8], 71), part)
    block_count = draw_block_count(jax.random.fold_in(arg_keys[8], 71), part)
    return {"probe_fine": probe_fine, "probe_coarse": probe_coarse, "kappa_fine": kappa_fine, "kappa_coarse": kappa_coarse, "phi_tiles": phi_tiles, "obs_weight": obs_weight, "block_index": block_index, "block_count": block_count}


def as_index(value):
    return jnp.asarray(value).astype(jnp.int32)


def apply_sar(field, kappa):
    padded = jnp.pad(field, ((0, 0), (1, 1), (1, 1)))
    beside_all = padded[:, 2:, 1:-1] + padded[:, :-2, 1:-1] + padded[:, 1:-1, 2:] + padded[:, 1:-1, :-2]
    return (4.0 + kappa) * field - beside_all


def observe(field_fine, field_coarse, phi_tiles, obs_weight, block_index, block_count):
    fine_ext = jnp.pad(field_fine, ((0, 0), (1, 1), (0, 0)))
    coarse_ext = jnp.pad(field_coarse, ((0, 0), (1, 1), (0, 0)))
    fine_count = (CX + 2) * (CY // TILE)
    tile_total = fine_count + CX // 2 + 2
    slots = jnp.arange(NB, dtype=jnp.int32)

    def one_device(carry, device):
        acc_fine, acc_coarse = carry
        east = device // N_NS
        north = device % N_NS
        zero = as_index(0)
        fine_start = (zero, as_index(east * CX), as_index(north * CY))
        coarse_start = (zero, as_index(east * (CX // 2)), as_index(north * (CY // 2)))
        tiles_fine = lax.dynamic_slice(fine_ext, fine_start, (P_SIZE, CX + 2, CY)).reshape(P_SIZE, fine_count, TILE)
        tiles_coarse = lax.dynamic_slice(coarse_ext, coarse_start, (P_SIZE, CX // 2 + 2, CY // 2))
        ext = jnp.concatenate([tiles_fine, tiles_coarse], axis=1)
        phi = lax.dynamic_slice_in_dim(phi_tiles, as_index(device * NB), NB, 0)
        index = lax.dynamic_slice_in_dim(block_index, as_index(device * NB), NB, 0)
        weights = lax.dynamic_slice_in_dim(obs_weight, as_index(device * NB), NB, 0)
        weights = weights * (slots < block_count[device]).astype(phi.dtype)[:, None]
        picked = ext[:, index]
        seen = jnp.einsum('bij,pbj->pbi', phi, picked, precision=lax.Precision.HIGHEST)
        scaled = seen * weights[None]
        back = jnp.einsum('bij,pbi->pbj', phi, scaled, precision=lax.Precision.HIGHEST)
        adjoint = jnp.zeros((P_SIZE, tile_total, TILE), phi.dtype).at[:, index].add(back)
        adj_fine = adjoint[:, :fine_count].reshape(P_SIZE, CX + 2, CY)
        adj_coarse = adjoint[:, fine_count:]
        acc_fine = lax.dynamic_update_slice(acc_fine, lax.dynamic_slice(acc_fine, fine_start, (P_SIZE, CX + 2, CY)) + adj_fine, fine_start)
        acc_coarse = lax.dynamic_update_slice(acc_coarse, lax.dynamic_slice(acc_coarse, coarse_start, (P_SIZE, CX // 2 + 2, CY // 2)) + adj_coarse, coarse_start)
        return (acc_fine, acc_coarse), None

    start_fine = jnp.zeros((P_SIZE, NX + 2, NY), field_fine.dtype)
    start_coarse = jnp.zeros((P_SIZE, NX // 2 + 2, NY // 2), field_coarse.dtype)
    (acc_fine, acc_coarse), _ = lax.scan(one_device, (start_fine, start_coarse), jnp.arange(N_EW * N_NS, dtype=jnp.int32))
    return acc_fine[:, 1:-1], acc_coarse[:, 1:-1]


def products(first_fine, first_coarse, second_fine, second_coarse):
    return jnp.sum(first_fine * second_fine, axis=(1, 2)) + jnp.sum(first_coarse * second_coarse, axis=(1, 2))


def reference(probe_fine, probe_coarse, kappa_fine, kappa_coarse, phi_tiles, obs_weight, block_index, block_count):
    def operator(field_fine, field_coarse):
        obs_fine, obs_coarse = observe(field_fine, field_coarse, phi_tiles, obs_weight, block_index, block_count)
        prior_fine = apply_sar(apply_sar(field_fine, kappa_fine), kappa_fine)
        prior_coarse = apply_sar(apply_sar(field_coarse, kappa_coarse), kappa_coarse)
        return prior_fine + obs_fine, prior_coarse + obs_coarse

    resid_fine = (2 * probe_fine - 1).astype(jnp.float32)
    resid_coarse = (2 * probe_coarse - 1).astype(jnp.float32)
    solve_fine = jnp.zeros_like(resid_fine)
    solve_coarse = jnp.zeros_like(resid_coarse)
    direction_fine, direction_coarse = resid_fine, resid_coarse
    norm_now = products(resid_fine, resid_coarse, resid_fine, resid_coarse)
    for iteration in range(ITERS):
        image_fine, image_coarse = operator(direction_fine, direction_coarse)
        alpha = (norm_now / products(direction_fine, direction_coarse, image_fine, image_coarse))[:, None, None]
        solve_fine = solve_fine + alpha * direction_fine
        solve_coarse = solve_coarse + alpha * direction_coarse
        resid_fine = resid_fine - alpha * image_fine
        resid_coarse = resid_coarse - alpha * image_coarse
        if iteration + 1 < ITERS:
            norm_next = products(resid_fine, resid_coarse, resid_fine, resid_coarse)
            ratio = (norm_next / norm_now)[:, None, None]
            direction_fine = resid_fine + ratio * direction_fine
            direction_coarse = resid_coarse + ratio * direction_coarse
            norm_now = norm_next
    return (solve_fine, solve_coarse, resid_fine, resid_coarse)
```

```python
import functools

import jax
import jax.numpy as jnp
from jax import lax
from jax.experimental import pallas as pl
from jax.experimental.pallas import tpu as pltpu
from jax.sharding import PartitionSpec as P

MESH = pl.DeviceIdType.MESH
CHUNKS = 16
GROUP = 8
F32 = jnp.float32
BF16 = jnp.bfloat16


def kernel(
    n_ew,
    n_ns,
    pf_ref,
    pc_ref,
    kf_ref,
    kc_ref,
    phi_ref,
    wt_ref,
    idxv_ref,
    cnt_ref,
    xf_ref,
    xc_ref,
    rf_ref,
    rc_ref,
    phi32,
    ph,
    z,
    u0,
    q1,
    u1,
    adj,
    im,
    ext,
    back,
    wm,
    onehot,
    pick,
    row_out,
    row_in,
    col_in,
    ar_out,
    ar_in,
    phi_sem,
    row_ssem,
    row_rsem,
    col_ssem,
    col_rsem,
    ar_ssem,
    ar_rsem,
):
    probes, rows, width = pf_ref.shape
    half_rows = pc_ref.shape[1]
    tile = pc_ref.shape[2]
    blocks = ph.shape[0]
    at = (8, rows + 24, rows + half_rows + 40)
    size = (rows, half_rows, rows)
    total = n_ew * n_ns
    e = lax.axis_index("ew")
    n = lax.axis_index("ns")
    me = e * n_ns + n
    has_row = (e > 0, e < n_ew - 1)
    has_col = (n > 0, n < n_ns - 1)
    row_dev = ({"ew": lax.max(e - 1, 0)}, {"ew": lax.min(e + 1, n_ew - 1)})
    col_dev = ({"ns": lax.max(n - 1, 0)}, {"ns": lax.min(n + 1, n_ns - 1)})

    def phi_copy(c):
        step = blocks // CHUNKS
        return pltpu.make_async_copy(
            phi_ref.at[pl.ds(c * step, step)], phi32.at[pl.ds(c * step, step)], phi_sem.at[c]
        )

    def start_phi(c, _):
        phi_copy(c).start()
        return 0

    lax.fori_loop(0, CHUNKS, start_phi, 0)

    def peer(k):
        other = lax.rem(me + k, total)
        return {"ew": other // n_ns, "ns": lax.rem(other, n_ns)}

    barrier = pltpu.get_barrier_semaphore()
    for k in range(1, total):
        pl.semaphore_signal(barrier, inc=1, device_id=peer(k), device_id_type=MESH)

    z[...] = jnp.zeros_like(z)
    u0[...] = jnp.zeros_like(u0)
    q1[...] = jnp.zeros_like(q1)
    u1[...] = jnp.zeros_like(u1)
    fine = (2 * pf_ref[...] - 1).astype(F32)
    z[:, at[0] : at[0] + rows, :] = fine[:, :, :tile]
    z[:, at[2] : at[2] + rows, :] = fine[:, :, tile:]
    z[:, at[1] : at[1] + half_rows, :] = (2 * pc_ref[...] - 1).astype(F32)
    row_out[...] = jnp.zeros_like(row_out)
    ar_out[...] = jnp.zeros_like(ar_out)
    for d in range(2):

        @pl.when(jnp.logical_not(has_row[d]))
        def _():
            for k in range(5):
                row_in[k, d] = jnp.zeros(row_in.shape[2:], F32)

        @pl.when(jnp.logical_not(has_col[d]))
        def _():
            for k in range(4):
                col_in[k, d] = jnp.zeros(col_in.shape[2:], F32)

    def row_copy(k, d):
        return pltpu.make_async_remote_copy(
            src_ref=row_out.at[k, d],
            dst_ref=row_in.at[k, 1 - d],
            send_sem=row_ssem.at[k, d],
            recv_sem=row_rsem.at[k, 1 - d],
            device_id=row_dev[d],
            device_id_type=MESH,
        )

    def row_start(k):
        for d in range(2):

            @pl.when(has_row[d])
            def _():
                row_copy(k, d).start()

    def row_wait(k):
        for d in range(2):

            @pl.when(has_row[d])
            def _():
                row_copy(k, 1 - d).wait_recv()

    def col_copies(field, k, d):
        seg = 0 if d == 0 else 2
        out = []
        for j, (s, first) in enumerate(((seg, 0), (1, rows))):
            out.append(
                pltpu.make_async_remote_copy(
                    src_ref=field.at[:, pl.ds(at[s], size[s]), :],
                    dst_ref=col_in.at[k, 1 - d, :, pl.ds(first, size[s]), :],
                    send_sem=col_ssem.at[k, d, j],
                    recv_sem=col_rsem.at[k, 1 - d, j],
                    device_id=col_dev[d],
                    device_id_type=MESH,
                )
            )
        return out

    def col_start(field, k):
        for d in range(2):

            @pl.when(has_col[d])
            def _():
                for c in col_copies(field, k, d):
                    c.start()

    def col_wait(field, k):
        for d in range(2):

            @pl.when(has_col[d])
            def _():
                for c in col_copies(field, k, 1 - d):
                    c.wait_recv()

    def pack_rows(field, k, first=0, outside=False):
        for s in range(3):
            low, high = at[s], at[s] + size[s] - 1
            if outside:
                low, high = low - 1, high + 1
            for p in range(probes):
                row_out[k, 0, s, pl.ds(first + p, 1), :] = field[p, pl.ds(low, 1), :]
                row_out[k, 1, s, pl.ds(first + p, 1), :] = field[p, pl.ds(high, 1), :]

    def unpack_rows(field, k):
        for s in range(3):
            for p in range(probes):
                field[p, pl.ds(at[s] - 1, 1), :] = row_in[k, 0, s, pl.ds(p, 1), :]
                field[p, pl.ds(at[s] + size[s], 1), :] = row_in[k, 1, s, pl.ds(p, 1), :]

    def sar(field, k, s, p):
        lane = lax.broadcasted_iota(jnp.int32, (size[s], tile), 1)

        def seg(which):
            return field[p, pl.ds(at[which], size[which]), :]

        first, last = (0, rows) if s != 1 else (rows, rows + half_rows)
        low = seg(0) if s == 2 else col_in[k, 0, p, first:last, :]
        high = seg(2) if s == 0 else col_in[k, 1, p, first:last, :]
        centre = seg(s)
        left = jnp.where(lane == 0, pltpu.roll(low, 1, 1), pltpu.roll(centre, 1, 1))
        right = jnp.where(
            lane == tile - 1, pltpu.roll(high, tile - 1, 1), pltpu.roll(centre, tile - 1, 1)
        )
        up = field[p, pl.ds(at[s] - 1, size[s]), :]
        down = field[p, pl.ds(at[s] + 1, size[s]), :]
        kap = kc_ref[...] if s == 1 else kf_ref[:, (s // 2) * tile : (s // 2 + 1) * tile]
        return (4.0 + kap) * centre - (down + up + right + left)

    def own(field, p, s):
        return field[p, pl.ds(at[s], size[s]), :]

    def put(field, p, s, value):
        field[p, pl.ds(at[s], size[s]), :] = value

    pl.semaphore_wait(barrier, total - 1)
    pack_rows(z, 0)
    row_start(0)
    col_start(z, 0)

    alive = lax.broadcasted_iota(jnp.int32, (blocks, tile), 0) < cnt_ref[0]
    wm[...] = jnp.where(alive, wt_ref[...], 0.0)
    line = lax.broadcasted_iota(jnp.int32, (z.shape[1], blocks), 0)
    per_row = width // tile
    name = jnp.where(
        line <= at[0] + rows,
        per_row * (line - (at[0] - 1)),
        jnp.where(
            line <= at[1] + half_rows,
            (rows + 2) * per_row + line - (at[1] - 1),
            per_row * (line - (at[2] - 1)) + 1,
        ),
    )
    inside = (
        ((line >= at[0] - 1) & (line <= at[0] + rows))
        | ((line >= at[1] - 1) & (line <= at[1] + half_rows))
        | ((line >= at[2] - 1) & (line <= at[2] + rows))
    )
    chosen = jnp.where(inside & (name == idxv_ref[...]), 1.0, 0.0)
    onehot[...] = chosen.astype(BF16)
    pick[...] = chosen.T.astype(BF16)

    def split_chunk(c, _):
        step = blocks // CHUNKS
        phi_copy(c).wait()
        for k in range(step):
            x = phi32[c * step + k]
            hi = x.astype(BF16)
            ph[c * step + k, 0:tile, :] = hi
            ph[c * step + k, tile : 2 * tile, :] = (x - hi.astype(F32)).astype(BF16)
        return 0

    lax.fori_loop(0, CHUNKS, split_chunk, 0)

    def fill_ext(field):
        for p in range(probes):
            x = field[p]
            hi = x.astype(BF16)
            lo = (x - hi.astype(F32)).astype(BF16)
            out = jnp.dot(
                pick[...], jnp.concatenate([hi, lo], axis=1), preferred_element_type=F32
            )
            ext[pl.ds(p, blocks, stride=8), :] = out[:, :tile]
            ext[pl.ds(4 + p, blocks, stride=8), :] = out[:, tile:]

    top = lax.broadcasted_iota(jnp.int32, (8, tile), 0) < 4

    def observe(g, _):
        scaled = []
        for k in range(GROUP):
            b = g * GROUP + k
            got = ext[pl.ds(pl.multiple_of(b * 8, 8), 8), :].astype(BF16)
            seen = lax.dot_general(
                got, ph[b], (((1,), (1,)), ((), ())), preferred_element_type=F32
            )
            seen = seen[:, :tile] + seen[:, tile:]
            seen = seen + pltpu.roll(seen, 4, 0)
            scaled.append(seen * wm[pl.ds(b, 1), :])
        for k in range(GROUP):
            b = g * GROUP + k
            hi = scaled[k].astype(BF16).astype(F32)
            parts = jnp.where(top, hi, scaled[k] - hi).astype(BF16)
            out = lax.dot_general(
                jnp.concatenate([parts, parts], axis=1),
                ph[b],
                (((1,), (0,)), ((), ())),
                preferred_element_type=F32,
            )
            back[pl.ds(pl.multiple_of(b * 8, 8), 8), :] = out + pltpu.roll(out, 4, 0)
        return 0

    steps = blocks // GROUP

    def scatter():
        for p in range(probes):
            x = back[pl.ds(p, blocks, stride=8), :]
            hi = x.astype(BF16)
            lo = (x - hi.astype(F32)).astype(BF16)
            out = jnp.dot(
                onehot[...], jnp.concatenate([hi, lo], axis=1), preferred_element_type=F32
            )
            adj[p] = out[:, :tile] + out[:, tile:]

    def ar_copy(k, j):
        return pltpu.make_async_remote_copy(
            src_ref=ar_out.at[k],
            dst_ref=ar_in.at[k, me],
            send_sem=ar_ssem.at[k, j],
            recv_sem=ar_rsem.at[k, me],
            device_id=peer(j),
            device_id_type=MESH,
        )

    def ar_recv(k, j):
        other = lax.rem(me + j, total)
        return pltpu.make_async_remote_copy(
            src_ref=ar_out.at[k],
            dst_ref=ar_in.at[k, other],
            send_sem=ar_ssem.at[k, j],
            recv_sem=ar_rsem.at[k, other],
            device_id=peer(j),
            device_id_type=MESH,
        )

    def ar_start(k):
        for j in range(1, total):
            ar_copy(k, j).start()
        ar_in[k, me] = ar_out[k]

    def ar_wait(k):
        for j in range(1, total):
            ar_recv(k, j).wait_recv()
        acc = ar_in[k, 0]
        for j in range(1, total):
            acc = acc + ar_in[k, j]
        return jnp.sum(acc, axis=1, keepdims=True)

    row_wait(0)
    unpack_rows(z, 0)
    col_wait(z, 0)
    for p in range(probes):
        for s in range(3):
            put(u0, p, s, sar(z, 0, s, p))
    pack_rows(u0, 1)
    row_start(1)
    col_start(u0, 1)
    fill_ext(z)
    lax.fori_loop(0, steps, observe, 0)
    scatter()
    row_wait(1)
    unpack_rows(u0, 1)
    col_wait(u0, 1)
    for p in range(probes):
        for s in range(3):
            put(q1, p, s, sar(u0, 1, s, p) + own(adj, p, s))
    pack_rows(q1, 2)
    pack_rows(adj, 2, first=4, outside=True)
    row_start(2)
    row_wait(2)
    mask = [jnp.where(h, 1.0, 0.0) for h in has_row]
    for s in range(3):
        edge = (at[s] - 1, at[s] + size[s])
        inner = (at[s], at[s] + size[s] - 1)
        for p in range(probes):
            for d in range(2):
                q1[p, pl.ds(edge[d], 1), :] = (
                    row_in[2, d, s, pl.ds(p, 1), :] + adj[p, pl.ds(edge[d], 1), :] * mask[d]
                )
                q1[p, pl.ds(inner[d], 1), :] = (
                    q1[p, pl.ds(inner[d], 1), :] + row_in[2, d, s, pl.ds(4 + p, 1), :]
                )
    col_start(q1, 2)

    def lanes(first, second, p):
        out = None
        for s in range(3):
            part = jnp.sum(first(p, s) * second(p, s), axis=0, keepdims=True)
            out = part if out is None else out + part
        return out

    own_z = functools.partial(own, z)
    own_q = functools.partial(own, q1)
    for p in range(probes):
        ar_out[0, pl.ds(p, 1), :] = lanes(own_z, own_z, p)
        ar_out[0, pl.ds(4 + p, 1), :] = lanes(own_z, own_q, p)
        ar_out[0, pl.ds(8 + p, 1), :] = lanes(own_q, own_q, p)
    ar_start(0)

    fill_ext(q1)
    lax.fori_loop(0, steps // 2, observe, 0)
    col_wait(q1, 2)
    for p in range(probes):
        for s in range(3):
            put(u1, p, s, sar(q1, 2, s, p))
    pack_rows(u1, 3)
    row_start(3)
    col_start(u1, 3)
    lax.fori_loop(steps // 2, steps, observe, 0)
    scatter()
    pack_rows(adj, 4, outside=True)
    row_start(4)
    row_wait(3)
    unpack_rows(u1, 3)
    col_wait(u1, 3)
    sums = ar_wait(0)
    rr, pq, qq = sums[0:4], sums[4:8], sums[8:12]
    alpha = rr / pq
    grow = alpha * (qq / pq)
    for p in range(probes):
        a1, g1 = alpha[p : p + 1], grow[p : p + 1]
        line_sum, norm_sum = None, None
        for s in range(3):
            image = g1 * own(q1, p, s) - a1 * (sar(u1, 3, s, p) + own(adj, p, s))
            direction = g1 * own(z, p, s) - a1 * own(q1, p, s)
            part = jnp.sum(direction * image, axis=0, keepdims=True)
            for d in range(2):
                edge = (at[s] - 1, at[s] + size[s])[d]
                outside = g1 * z[p, pl.ds(edge, 1), :] - a1 * q1[p, pl.ds(edge, 1), :]
                part = part - a1 * (outside * adj[p, pl.ds(edge, 1), :]) * mask[d]
            line_sum = part if line_sum is None else line_sum + part
            resid = own(z, p, s) - a1 * own(q1, p, s)
            part = jnp.sum(resid * resid, axis=0, keepdims=True)
            norm_sum = part if norm_sum is None else norm_sum + part
            put(im, p, s, image)
        ar_out[1, pl.ds(p, 1), :] = line_sum
        ar_out[1, pl.ds(4 + p, 1), :] = norm_sum
    ar_start(1)

    row_wait(4)
    for s in range(3):
        inner = (at[s], at[s] + size[s] - 1)
        for p in range(probes):
            for d in range(2):
                im[p, pl.ds(inner[d], 1), :] = (
                    im[p, pl.ds(inner[d], 1), :]
                    - alpha[p : p + 1] * row_in[4, d, s, pl.ds(p, 1), :]
                )
    last = ar_wait(1)
    alpha_two = last[4:8] / last[0:4]
    for p in range(probes):
        a1, g1, a2 = alpha[p : p + 1], grow[p : p + 1], alpha_two[p : p + 1]
        for s in range(3):
            zz, qq_ = own(z, p, s), own(q1, p, s)
            solve = a1 * zz + a2 * (g1 * zz - a1 * qq_)
            resid = zz - a1 * qq_ - a2 * own(im, p, s)
            if s == 1:
                xc_ref[p] = solve
                rc_ref[p] = resid
            else:
                columns = slice((s // 2) * tile, (s // 2 + 1) * tile)
                xf_ref[p, :, columns] = solve
                rf_ref[p, :, columns] = resid
    for k in range(5):
        for d in range(2):

            @pl.when(has_row[d])
            def _():
                row_copy(k, d).wait_send()

    for k, field in enumerate((z, u0, q1, u1)):
        for d in range(2):

            @pl.when(has_col[d])
            def _():
                for c in col_copies(field, k, d):
                    c.wait_send()

    for k in range(2):
        for j in range(1, total):
            ar_copy(k, j).wait_send()


def local(
    n_ew,
    n_ns,
    probe_fine,
    probe_coarse,
    kappa_fine,
    kappa_coarse,
    phi_tiles,
    obs_weight,
    block_index,
    block_count,
):
    probes, rows, width = probe_fine.shape
    half_rows, tile = probe_coarse.shape[1:]
    blocks = phi_tiles.shape[0]
    lines = 2 * rows + half_rows + 48
    total = n_ew * n_ns
    vmem = pl.BlockSpec(memory_space=pltpu.VMEM)
    smem = pl.BlockSpec(memory_space=pltpu.SMEM)
    field = pltpu.VMEM((probes, lines, tile), F32)
    dma = pltpu.SemaphoreType.DMA
    return pl.pallas_call(
        functools.partial(kernel, n_ew, n_ns),
        out_shape=(
            jax.ShapeDtypeStruct(probe_fine.shape, F32),
            jax.ShapeDtypeStruct(probe_coarse.shape, F32),
            jax.ShapeDtypeStruct(probe_fine.shape, F32),
            jax.ShapeDtypeStruct(probe_coarse.shape, F32),
        ),
        in_specs=[vmem] * 4 + [pl.BlockSpec(memory_space=pl.ANY), vmem, vmem, smem],
        out_specs=(vmem,) * 4,
        scratch_shapes=[
            pltpu.VMEM(phi_tiles.shape, F32),
            pltpu.VMEM((blocks, 2 * tile, tile), BF16),
            field,
            field,
            field,
            field,
            field,
            field,
            pltpu.VMEM((blocks * 8, tile), F32),
            pltpu.VMEM((blocks * 8, tile), F32),
            pltpu.VMEM((blocks, tile), F32),
            pltpu.VMEM((lines, blocks), BF16),
            pltpu.VMEM((blocks, lines), BF16),
            pltpu.VMEM((5, 2, 3, 8, tile), F32),
            pltpu.VMEM((5, 2, 3, 8, tile), F32),
            pltpu.VMEM((4, 2, probes, rows + half_rows, tile), F32),
            pltpu.VMEM((2, 16, tile), F32),
            pltpu.VMEM((2, total, 16, tile), F32),
            dma((CHUNKS,)),
            dma((5, 2)),
            dma((5, 2)),
            dma((4, 2, 2)),
            dma((4, 2, 2)),
            dma((2, total)),
            dma((2, total)),
        ],
        compiler_params=pltpu.CompilerParams(
            collective_id=0, has_side_effects=True, vmem_limit_bytes=40 * 2**20
        ),
        cost_estimate=pl.CostEstimate(
            flops=4 * blocks * tile * tile * 8 * 4, bytes_accessed=phi_tiles.size * 4, transcendentals=0
        ),
    )(
        probe_fine,
        probe_coarse,
        kappa_fine,
        kappa_coarse,
        phi_tiles,
        obs_weight,
        block_index.reshape(1, blocks),
        block_count,
    )


def solution(mesh):
    in_specs = (
        P("lvl", "ew", "ns"),
        P("lvl", "ew", "ns"),
        P(("grp", "ew"), "ns"),
        P(("grp", "ew"), "ns"),
        P(("ew", "ns"), None, None),
        P(("grp", "ew", "ns"), None),
        P(("ew", "ns")),
        P(("ew", "ns")),
    )
    out_specs = (P(("grp", "lvl"), "ew", "ns"),) * 4
    body = functools.partial(local, mesh.shape["ew"], mesh.shape["ns"])
    return jax.shard_map(body, mesh=mesh, in_specs=in_specs, out_specs=out_specs, check_vma=False)
```

```python
import functools

import jax
import jax.numpy as jnp
from jax import lax
from jax.experimental import pallas as pl
from jax.experimental.pallas import tpu as pltpu
from jax.sharding import PartitionSpec as P

MESH = pl.DeviceIdType.MESH
CHUNKS = 16
GROUP = 16
VMEM_BYTES = 64 * 2**20 - 2**16
F32 = jnp.float32
BF16 = jnp.bfloat16


def kernel(
    n_ew,
    n_ns,
    pf_hbm,
    pc_hbm,
    kf_hbm,
    kc_hbm,
    phi_ref,
    wt_hbm,
    idxv_hbm,
    cnt_ref,
    xf_ref,
    xc_ref,
    rf_ref,
    rc_ref,
    pf_ref,
    pc_ref,
    kf_ref,
    kc_ref,
    wt_ref,
    idxv_ref,
    phi32,
    ph,
    z,
    u0,
    q1,
    u1,
    adj,
    im,
    ext,
    back,
    wm,
    onehot,
    pick,
    row_out,
    row_in,
    col_in,
    ar_out,
    ar_in,
    in_sem,
    phi_sem,
    row_ssem,
    row_rsem,
    col_ssem,
    col_rsem,
    ar_ssem,
    ar_rsem,
):
    probes, rows, width = pf_ref.shape
    half_rows = pc_ref.shape[1]
    tile = pc_ref.shape[2]
    blocks = ph.shape[0]
    at = (8, rows + 24, rows + half_rows + 40)
    size = (rows, half_rows, rows)
    total = n_ew * n_ns
    e = lax.axis_index("ew")
    n = lax.axis_index("ns")
    me = e * n_ns + n
    has_row = (e > 0, e < n_ew - 1)
    has_col = (n > 0, n < n_ns - 1)
    row_dev = ({"ew": lax.max(e - 1, 0)}, {"ew": lax.min(e + 1, n_ew - 1)})
    col_dev = ({"ns": lax.max(n - 1, 0)}, {"ns": lax.min(n + 1, n_ns - 1)})

    def input_copy(k):
        source, target = (
            (pf_hbm, pf_ref),
            (pc_hbm, pc_ref),
            (wt_hbm, wt_ref),
            (idxv_hbm, idxv_ref),
            (kf_hbm, kf_ref),
            (kc_hbm, kc_ref),
        )[k]
        return pltpu.make_async_copy(source, target, in_sem.at[k])

    for k in range(6):
        input_copy(k).start()

    def phi_copy(c):
        step = blocks // CHUNKS
        return pltpu.make_async_copy(
            phi_ref.at[pl.ds(c * step, step)], phi32.at[pl.ds(c * step, step)], phi_sem.at[c]
        )

    def start_phi(c, _):
        phi_copy(c).start()
        return 0

    lax.fori_loop(0, CHUNKS, start_phi, 0)

    def peer(k):
        other = lax.rem(me + k, total)
        return {"ew": other // n_ns, "ns": lax.rem(other, n_ns)}

    barrier = pltpu.get_barrier_semaphore()
    for k in range(1, total):
        pl.semaphore_signal(barrier, inc=1, device_id=peer(k), device_id_type=MESH)

    z[...] = jnp.zeros_like(z)
    u0[...] = jnp.zeros_like(u0)
    q1[...] = jnp.zeros_like(q1)
    u1[...] = jnp.zeros_like(u1)
    row_out[...] = jnp.zeros_like(row_out)
    ar_out[...] = jnp.zeros_like(ar_out)
    for d in range(2):

        @pl.when(jnp.logical_not(has_row[d]))
        def _():
            for k in range(5):
                row_in[k, d] = jnp.zeros(row_in.shape[2:], F32)

        @pl.when(jnp.logical_not(has_col[d]))
        def _():
            for k in range(4):
                col_in[k, d] = jnp.zeros(col_in.shape[2:], F32)

    def row_copy(k, d):
        return pltpu.make_async_remote_copy(
            src_ref=row_out.at[k, d],
            dst_ref=row_in.at[k, 1 - d],
            send_sem=row_ssem.at[k, d],
            recv_sem=row_rsem.at[k, 1 - d],
            device_id=row_dev[d],
            device_id_type=MESH,
        )

    def row_start(k):
        for d in range(2):

            @pl.when(has_row[d])
            def _():
                row_copy(k, d).start()

    def row_wait(k):
        for d in range(2):

            @pl.when(has_row[d])
            def _():
                row_copy(k, 1 - d).wait_recv()

    def col_copies(field, k, d):
        seg = 0 if d == 0 else 2
        out = []
        for j, (s, first) in enumerate(((seg, 0), (1, rows))):
            out.append(
                pltpu.make_async_remote_copy(
                    src_ref=field.at[:, pl.ds(at[s], size[s]), :],
                    dst_ref=col_in.at[k, 1 - d, :, pl.ds(first, size[s]), :],
                    send_sem=col_ssem.at[k, d, j],
                    recv_sem=col_rsem.at[k, 1 - d, j],
                    device_id=col_dev[d],
                    device_id_type=MESH,
                )
            )
        return out

    def col_start(field, k):
        for d in range(2):

            @pl.when(has_col[d])
            def _():
                for c in col_copies(field, k, d):
                    c.start()

    def col_wait(field, k):
        for d in range(2):

            @pl.when(has_col[d])
            def _():
                for c in col_copies(field, k, 1 - d):
                    c.wait_recv()

    def pack_rows(field, k, first=0, outside=False):
        for s in range(3):
            low, high = at[s], at[s] + size[s] - 1
            if outside:
                low, high = low - 1, high + 1
            for p in range(probes):
                row_out[k, 0, s, pl.ds(first + p, 1), :] = field[p, pl.ds(low, 1), :]
                row_out[k, 1, s, pl.ds(first + p, 1), :] = field[p, pl.ds(high, 1), :]

    def unpack_rows(field, k):
        for s in range(3):
            for p in range(probes):
                field[p, pl.ds(at[s] - 1, 1), :] = row_in[k, 0, s, pl.ds(p, 1), :]
                field[p, pl.ds(at[s] + size[s], 1), :] = row_in[k, 1, s, pl.ds(p, 1), :]

    def sar(field, k, s, p):
        lane = lax.broadcasted_iota(jnp.int32, (size[s], tile), 1)

        def seg(which):
            return field[p, pl.ds(at[which], size[which]), :]

        first, last = (0, rows) if s != 1 else (rows, rows + half_rows)
        low = seg(0) if s == 2 else col_in[k, 0, p, first:last, :]
        high = seg(2) if s == 0 else col_in[k, 1, p, first:last, :]
        centre = seg(s)
        left = jnp.where(lane == 0, pltpu.roll(low, 1, 1), pltpu.roll(centre, 1, 1))
        right = jnp.where(
            lane == tile - 1, pltpu.roll(high, tile - 1, 1), pltpu.roll(centre, tile - 1, 1)
        )
        up = field[p, pl.ds(at[s] - 1, size[s]), :]
        down = field[p, pl.ds(at[s] + 1, size[s]), :]
        kap = kc_ref[...] if s == 1 else kf_ref[:, (s // 2) * tile : (s // 2 + 1) * tile]
        return (4.0 + kap) * centre - (down + up + right + left)

    def own(field, p, s):
        return field[p, pl.ds(at[s], size[s]), :]

    def put(field, p, s, value):
        field[p, pl.ds(at[s], size[s]), :] = value

    input_copy(0).wait()
    input_copy(1).wait()
    fine = (2 * pf_ref[...] - 1).astype(F32)
    z[:, at[0] : at[0] + rows, :] = fine[:, :, :tile]
    z[:, at[2] : at[2] + rows, :] = fine[:, :, tile:]
    z[:, at[1] : at[1] + half_rows, :] = (2 * pc_ref[...] - 1).astype(F32)
    pl.semaphore_wait(barrier, total - 1)
    pack_rows(z, 0)
    row_start(0)
    col_start(z, 0)

    for k in range(2, 6):
        input_copy(k).wait()
    alive = lax.broadcasted_iota(jnp.int32, (blocks, tile), 0) < cnt_ref[0]
    wm[...] = jnp.where(alive, wt_ref[...], 0.0)
    line = lax.broadcasted_iota(jnp.int32, (z.shape[1], blocks), 0)
    per_row = width // tile
    name = jnp.where(
        line <= at[0] + rows,
        per_row * (line - (at[0] - 1)),
        jnp.where(
            line <= at[1] + half_rows,
            (rows + 2) * per_row + line - (at[1] - 1),
            per_row * (line - (at[2] - 1)) + 1,
        ),
    )
    inside = (
        ((line >= at[0] - 1) & (line <= at[0] + rows))
        | ((line >= at[1] - 1) & (line <= at[1] + half_rows))
        | ((line >= at[2] - 1) & (line <= at[2] + rows))
    )
    chosen = jnp.where(inside & (name == idxv_ref[...]), 1.0, 0.0)
    onehot[...] = chosen.astype(BF16)
    pick[...] = chosen.T.astype(BF16)

    def split_chunk(c, _):
        step = blocks // CHUNKS
        phi_copy(c).wait()
        for k in range(step):
            x = phi32[c * step + k]
            hi = x.astype(BF16)
            ph[c * step + k, 0:tile, :] = hi
            ph[c * step + k, tile : 2 * tile, :] = (x - hi.astype(F32)).astype(BF16)
        return 0

    lax.fori_loop(0, CHUNKS, split_chunk, 0)

    def fill_ext(field):
        for p in range(probes):
            x = field[p]
            hi = x.astype(BF16)
            lo = (x - hi.astype(F32)).astype(BF16)
            out = jnp.dot(
                pick[...], jnp.concatenate([hi, lo], axis=1), preferred_element_type=F32
            )
            ext[pl.ds(p, blocks, stride=8), :] = out[:, :tile]
            ext[pl.ds(4 + p, blocks, stride=8), :] = out[:, tile:]

    top = lax.broadcasted_iota(jnp.int32, (8, tile), 0) < 4

    def observe(g, _):
        scaled = []
        for k in range(GROUP):
            b = g * GROUP + k
            got = ext[pl.ds(pl.multiple_of(b * 8, 8), 8), :].astype(BF16)
            seen = lax.dot_general(
                got, ph[b], (((1,), (1,)), ((), ())), preferred_element_type=F32
            )
            seen = seen[:, :tile] + seen[:, tile:]
            seen = seen + pltpu.roll(seen, 4, 0)
            scaled.append(seen * wm[pl.ds(b, 1), :])
        for k in range(GROUP):
            b = g * GROUP + k
            hi = scaled[k].astype(BF16).astype(F32)
            parts = jnp.where(top, hi, scaled[k] - hi).astype(BF16)
            out = lax.dot_general(
                jnp.concatenate([parts, parts], axis=1),
                ph[b],
                (((1,), (0,)), ((), ())),
                preferred_element_type=F32,
            )
            back[pl.ds(pl.multiple_of(b * 8, 8), 8), :] = out + pltpu.roll(out, 4, 0)
        return 0

    steps = blocks // GROUP

    def scatter():
        for p in range(probes):
            x = back[pl.ds(p, blocks, stride=8), :]
            hi = x.astype(BF16)
            lo = (x - hi.astype(F32)).astype(BF16)
            out = jnp.dot(
                onehot[...], jnp.concatenate([hi, lo], axis=1), preferred_element_type=F32
            )
            adj[p] = out[:, :tile] + out[:, tile:]

    def ar_copy(k, j):
        return pltpu.make_async_remote_copy(
            src_ref=ar_out.at[k],
            dst_ref=ar_in.at[k, me],
            send_sem=ar_ssem.at[k, j],
            recv_sem=ar_rsem.at[k, me],
            device_id=peer(j),
            device_id_type=MESH,
        )

    def ar_recv(k, j):
        other = lax.rem(me + j, total)
        return pltpu.make_async_remote_copy(
            src_ref=ar_out.at[k],
            dst_ref=ar_in.at[k, other],
            send_sem=ar_ssem.at[k, j],
            recv_sem=ar_rsem.at[k, other],
            device_id=peer(j),
            device_id_type=MESH,
        )

    def ar_start(k):
        for j in range(1, total):
            ar_copy(k, j).start()
        ar_in[k, me] = ar_out[k]

    def ar_wait(k):
        for j in range(1, total):
            ar_recv(k, j).wait_recv()
        acc = ar_in[k, 0]
        for j in range(1, total):
            acc = acc + ar_in[k, j]
        return jnp.sum(acc, axis=1, keepdims=True)

    row_wait(0)
    unpack_rows(z, 0)
    col_wait(z, 0)
    for p in range(probes):
        for s in range(3):
            put(u0, p, s, sar(z, 0, s, p))
    pack_rows(u0, 1)
    row_start(1)
    col_start(u0, 1)
    fill_ext(z)
    lax.fori_loop(0, steps, observe, 0)
    scatter()
    row_wait(1)
    unpack_rows(u0, 1)
    col_wait(u0, 1)
    for p in range(probes):
        for s in range(3):
            put(q1, p, s, sar(u0, 1, s, p) + own(adj, p, s))
    pack_rows(q1, 2)
    pack_rows(adj, 2, first=4, outside=True)
    row_start(2)
    row_wait(2)
    mask = [jnp.where(h, 1.0, 0.0) for h in has_row]
    for s in range(3):
        edge = (at[s] - 1, at[s] + size[s])
        inner = (at[s], at[s] + size[s] - 1)
        for p in range(probes):
            for d in range(2):
                q1[p, pl.ds(edge[d], 1), :] = (
                    row_in[2, d, s, pl.ds(p, 1), :] + adj[p, pl.ds(edge[d], 1), :] * mask[d]
                )
                q1[p, pl.ds(inner[d], 1), :] = (
                    q1[p, pl.ds(inner[d], 1), :] + row_in[2, d, s, pl.ds(4 + p, 1), :]
                )
    col_start(q1, 2)

    def lanes(first, second, p):
        out = None
        for s in range(3):
            part = jnp.sum(first(p, s) * second(p, s), axis=0, keepdims=True)
            out = part if out is None else out + part
        return out

    own_z = functools.partial(own, z)
    own_q = functools.partial(own, q1)
    for p in range(probes):
        ar_out[0, pl.ds(p, 1), :] = lanes(own_z, own_z, p)
        ar_out[0, pl.ds(4 + p, 1), :] = lanes(own_z, own_q, p)
        ar_out[0, pl.ds(8 + p, 1), :] = lanes(own_q, own_q, p)
    ar_start(0)

    fill_ext(q1)
    lax.fori_loop(0, steps // 2, observe, 0)
    col_wait(q1, 2)
    for p in range(probes):
        for s in range(3):
            put(u1, p, s, sar(q1, 2, s, p))
    pack_rows(u1, 3)
    row_start(3)
    col_start(u1, 3)
    lax.fori_loop(steps // 2, steps, observe, 0)
    scatter()
    pack_rows(adj, 4, outside=True)
    row_start(4)
    row_wait(3)
    unpack_rows(u1, 3)
    col_wait(u1, 3)
    sums = ar_wait(0)
    rr, pq, qq = sums[0:4], sums[4:8], sums[8:12]
    alpha = rr / pq
    grow = alpha * (qq / pq)
    for p in range(probes):
        a1, g1 = alpha[p : p + 1], grow[p : p + 1]
        line_sum, norm_sum = None, None
        for s in range(3):
            image = g1 * own(q1, p, s) - a1 * (sar(u1, 3, s, p) + own(adj, p, s))
            direction = g1 * own(z, p, s) - a1 * own(q1, p, s)
            part = jnp.sum(direction * image, axis=0, keepdims=True)
            for d in range(2):
                edge = (at[s] - 1, at[s] + size[s])[d]
                outside = g1 * z[p, pl.ds(edge, 1), :] - a1 * q1[p, pl.ds(edge, 1), :]
                part = part - a1 * (outside * adj[p, pl.ds(edge, 1), :]) * mask[d]
            line_sum = part if line_sum is None else line_sum + part
            resid = own(z, p, s) - a1 * own(q1, p, s)
            part = jnp.sum(resid * resid, axis=0, keepdims=True)
            norm_sum = part if norm_sum is None else norm_sum + part
            put(im, p, s, image)
        ar_out[1, pl.ds(p, 1), :] = line_sum
        ar_out[1, pl.ds(4 + p, 1), :] = norm_sum
    ar_start(1)

    row_wait(4)
    for s in range(3):
        inner = (at[s], at[s] + size[s] - 1)
        for p in range(probes):
            for d in range(2):
                im[p, pl.ds(inner[d], 1), :] = (
                    im[p, pl.ds(inner[d], 1), :]
                    - alpha[p : p + 1] * row_in[4, d, s, pl.ds(p, 1), :]
                )
    last = ar_wait(1)
    alpha_two = last[4:8] / last[0:4]
    for p in range(probes):
        a1, g1, a2 = alpha[p : p + 1], grow[p : p + 1], alpha_two[p : p + 1]
        for s in range(3):
            zz, qq_ = own(z, p, s), own(q1, p, s)
            solve = a1 * zz + a2 * (g1 * zz - a1 * qq_)
            resid = zz - a1 * qq_ - a2 * own(im, p, s)
            if s == 1:
                xc_ref[p] = solve
                rc_ref[p] = resid
            else:
                columns = slice((s // 2) * tile, (s // 2 + 1) * tile)
                xf_ref[p, :, columns] = solve
                rf_ref[p, :, columns] = resid
    for k in range(5):
        for d in range(2):

            @pl.when(has_row[d])
            def _():
                row_copy(k, d).wait_send()

    for k, field in enumerate((z, u0, q1, u1)):
        for d in range(2):

            @pl.when(has_col[d])
            def _():
                for c in col_copies(field, k, d):
                    c.wait_send()

    for k in range(2):
        for j in range(1, total):
            ar_copy(k, j).wait_send()


def write_out(*refs):
    sources, targets, sem = refs[:4], refs[4:8], refs[8]
    copies = [pltpu.make_async_copy(sources[k], targets[k], sem.at[k]) for k in range(4)]
    for copy in copies:
        copy.start()
    for copy in copies:
        copy.wait()


def local(
    n_ew,
    n_ns,
    probe_fine,
    probe_coarse,
    kappa_fine,
    kappa_coarse,
    phi_tiles,
    obs_weight,
    block_index,
    block_count,
):
    probes, rows, width = probe_fine.shape
    half_rows, tile = probe_coarse.shape[1:]
    blocks = phi_tiles.shape[0]
    lines = 2 * rows + half_rows + 48
    total = n_ew * n_ns
    vmem = pl.BlockSpec(memory_space=pltpu.VMEM)
    smem = pl.BlockSpec(memory_space=pltpu.SMEM)
    field = pltpu.VMEM((probes, lines, tile), F32)
    dma = pltpu.SemaphoreType.DMA
    results = pl.pallas_call(
        functools.partial(kernel, n_ew, n_ns),
        out_shape=(
            jax.ShapeDtypeStruct(probe_fine.shape, F32),
            jax.ShapeDtypeStruct(probe_coarse.shape, F32),
            jax.ShapeDtypeStruct(probe_fine.shape, F32),
            jax.ShapeDtypeStruct(probe_coarse.shape, F32),
        ),
        in_specs=[pl.BlockSpec(memory_space=pltpu.HBM)] * 7 + [smem],
        out_specs=(vmem,) * 4,
        scratch_shapes=[
            pltpu.VMEM(probe_fine.shape, jnp.int32),
            pltpu.VMEM(probe_coarse.shape, jnp.int32),
            pltpu.VMEM(kappa_fine.shape, F32),
            pltpu.VMEM(kappa_coarse.shape, F32),
            pltpu.VMEM(obs_weight.shape, F32),
            pltpu.VMEM((1, blocks), jnp.int32),
            pltpu.VMEM(phi_tiles.shape, F32),
            pltpu.VMEM((blocks, 2 * tile, tile), BF16),
            field,
            field,
            field,
            field,
            field,
            field,
            pltpu.VMEM((blocks * 8, tile), F32),
            pltpu.VMEM((blocks * 8, tile), F32),
            pltpu.VMEM((blocks, tile), F32),
            pltpu.VMEM((lines, blocks), BF16),
            pltpu.VMEM((blocks, lines), BF16),
            pltpu.VMEM((5, 2, 3, 8, tile), F32),
            pltpu.VMEM((5, 2, 3, 8, tile), F32),
            pltpu.VMEM((4, 2, probes, rows + half_rows, tile), F32),
            pltpu.VMEM((2, 16, tile), F32),
            pltpu.VMEM((2, total, 16, tile), F32),
            dma((6,)),
            dma((CHUNKS,)),
            dma((5, 2)),
            dma((5, 2)),
            dma((4, 2, 2)),
            dma((4, 2, 2)),
            dma((2, total)),
            dma((2, total)),
        ],
        compiler_params=pltpu.CompilerParams(
            collective_id=0, has_side_effects=True, vmem_limit_bytes=VMEM_BYTES
        ),
        cost_estimate=pl.CostEstimate(
            flops=4 * blocks * tile * tile * 8 * 4, bytes_accessed=phi_tiles.size * 4, transcendentals=0
        ),
    )(
        probe_fine,
        probe_coarse,
        kappa_fine,
        kappa_coarse,
        phi_tiles,
        obs_weight,
        block_index.reshape(1, blocks),
        block_count,
    )
    return pl.pallas_call(
        write_out,
        out_shape=tuple(jax.ShapeDtypeStruct(r.shape, F32) for r in results),
        in_specs=[vmem] * 4,
        out_specs=(pl.BlockSpec(memory_space=pltpu.HBM),) * 4,
        scratch_shapes=[dma((4,))],
    )(*results)


def solution(mesh):
    in_specs = (
        P("lvl", "ew", "ns"),
        P("lvl", "ew", "ns"),
        P(("grp", "ew"), "ns"),
        P(("grp", "ew"), "ns"),
        P(("ew", "ns"), None, None),
        P(("grp", "ew", "ns"), None),
        P(("ew", "ns")),
        P(("ew", "ns")),
    )
    out_specs = (P(("grp", "lvl"), "ew", "ns"),) * 4
    body = functools.partial(local, mesh.shape["ew"], mesh.shape["ns"])
    return jax.shard_map(body, mesh=mesh, in_specs=in_specs, out_specs=out_specs, check_vma=False)
```

```python
import functools

import jax
import jax.numpy as jnp
from jax import lax
from jax.experimental import pallas as pl
from jax.experimental.pallas import tpu as pltpu
from jax.sharding import PartitionSpec as P

MESH = pl.DeviceIdType.MESH
GROUP = 32
VMEM_BYTES = 64 * 2**20 - 2**16
F32 = jnp.float32
BF16 = jnp.bfloat16


def kernel(
    n_ew,
    n_ns,
    pf_hbm,
    pc_hbm,
    kf_hbm,
    kc_hbm,
    phi_ref,
    wt_hbm,
    idxv_hbm,
    cnt_ref,
    xf_ref,
    xc_ref,
    rf_ref,
    rc_ref,
    pf_ref,
    pc_ref,
    kf_ref,
    kc_ref,
    wt_ref,
    idxv_ref,
    phi32,
    ph,
    z,
    u0,
    q1,
    u1,
    adj,
    im,
    ext,
    back,
    wm,
    onehot,
    pick,
    row_out,
    row_in,
    col_out,
    col_in,
    ar_out,
    ar_in,
    in_sem,
    phi_sem,
    row_ssem,
    row_rsem,
    col_ssem,
    col_rsem,
    ar_ssem,
    ar_rsem,
):
    probes, rows, width = pf_ref.shape
    half_rows = pc_ref.shape[1]
    tile = pc_ref.shape[2]
    blocks = ph.shape[0]
    at = (8, rows + 24, rows + half_rows + 40)
    size = (rows, half_rows, rows)
    chunks = blocks // GROUP
    total = n_ew * n_ns
    e = lax.axis_index("ew")
    n = lax.axis_index("ns")
    me = e * n_ns + n
    has_row = (e > 0, e < n_ew - 1)
    has_col = (n > 0, n < n_ns - 1)
    row_dev = ({"ew": lax.max(e - 1, 0)}, {"ew": lax.min(e + 1, n_ew - 1)})
    col_dev = ({"ns": lax.max(n - 1, 0)}, {"ns": lax.min(n + 1, n_ns - 1)})

    def input_copy(k):
        source, target = (
            (pf_hbm, pf_ref),
            (pc_hbm, pc_ref),
            (wt_hbm, wt_ref),
            (idxv_hbm, idxv_ref),
            (kf_hbm, kf_ref),
            (kc_hbm, kc_ref),
        )[k]
        return pltpu.make_async_copy(source, target, in_sem.at[k])

    for k in range(6):
        input_copy(k).start()

    def phi_copy(c):
        part = pl.ds(c * GROUP, GROUP)
        return pltpu.make_async_copy(phi_ref.at[part], phi32.at[part], phi_sem.at[c]
        )

    def start_phi(c, _):
        phi_copy(c).start()
        return 0

    lax.fori_loop(0, chunks, start_phi, 0)

    def peer(k):
        other = lax.rem(me + k, total)
        return {"ew": other // n_ns, "ns": lax.rem(other, n_ns)}

    barrier = pltpu.get_barrier_semaphore()
    for k in range(1, total):
        pl.semaphore_signal(barrier, inc=1, device_id=peer(k), device_id_type=MESH)

    z[...] = jnp.zeros_like(z)
    u0[...] = jnp.zeros_like(u0)
    q1[...] = jnp.zeros_like(q1)
    u1[...] = jnp.zeros_like(u1)
    row_out[...] = jnp.zeros_like(row_out)
    ar_out[...] = jnp.zeros_like(ar_out)
    for d in range(2):

        @pl.when(jnp.logical_not(has_row[d]))
        def _():
            for k in range(5):
                row_in[k, d] = jnp.zeros(row_in.shape[2:], F32)

        @pl.when(jnp.logical_not(has_col[d]))
        def _():
            for k in range(4):
                col_in[k, d] = jnp.zeros(col_in.shape[2:], F32)

    def row_copy(k, d):
        return pltpu.make_async_remote_copy(
            src_ref=row_out.at[k, d],
            dst_ref=row_in.at[k, 1 - d],
            send_sem=row_ssem.at[k, d],
            recv_sem=row_rsem.at[k, 1 - d],
            device_id=row_dev[d],
            device_id_type=MESH,
        )

    def row_start(k):
        for d in range(2):

            @pl.when(has_row[d])
            def _():
                row_copy(k, d).start()

    def row_wait(k):
        for d in range(2):

            @pl.when(has_row[d])
            def _():
                row_copy(k, 1 - d).wait_recv()

    def turned(x, distance):
        return pltpu.roll(x, distance % tile, 1) if distance % tile else x

    def pack_cols(field, k):
        for d in range(2):
            edge = (0, tile - 1)[d]
            for s, first in ((2 * d, 0), (1, rows)):
                lane = lax.broadcasted_iota(jnp.int32, (size[s], tile), 1)
                packed = jnp.zeros((size[s], tile), F32)
                for p in range(probes):
                    moved = turned(field[p, pl.ds(at[s], size[s]), :], p - edge)
                    packed = jnp.where(lane == p, moved, packed)
                col_out[k, d, pl.ds(first, size[s]), :] = packed

    def col_copy(k, d):
        return pltpu.make_async_remote_copy(
            src_ref=col_out.at[k, d],
            dst_ref=col_in.at[k, 1 - d],
            send_sem=col_ssem.at[k, d],
            recv_sem=col_rsem.at[k, 1 - d],
            device_id=col_dev[d],
            device_id_type=MESH,
        )

    def col_start(field, k):
        pack_cols(field, k)
        for d in range(2):

            @pl.when(has_col[d])
            def _():
                col_copy(k, d).start()

    def col_wait(k):
        for d in range(2):

            @pl.when(has_col[d])
            def _():
                col_copy(k, 1 - d).wait_recv()

    def pack_rows(field, k, first=0, outside=False):
        for s in range(3):
            low, high = at[s], at[s] + size[s] - 1
            if outside:
                low, high = low - 1, high + 1
            for p in range(probes):
                row_out[k, 0, s, pl.ds(first + p, 1), :] = field[p, pl.ds(low, 1), :]
                row_out[k, 1, s, pl.ds(first + p, 1), :] = field[p, pl.ds(high, 1), :]

    def unpack_rows(field, k):
        for s in range(3):
            for p in range(probes):
                field[p, pl.ds(at[s] - 1, 1), :] = row_in[k, 0, s, pl.ds(p, 1), :]
                field[p, pl.ds(at[s] + size[s], 1), :] = row_in[k, 1, s, pl.ds(p, 1), :]

    def sar(field, k, s, p):
        lane = lax.broadcasted_iota(jnp.int32, (size[s], tile), 1)

        def seg(which):
            return field[p, pl.ds(at[which], size[which]), :]

        first, last = (0, rows) if s != 1 else (rows, rows + half_rows)
        low = turned(seg(0), 1) if s == 2 else turned(col_in[k, 0, first:last, :], -p)
        high = turned(seg(2), -1) if s == 0 else turned(col_in[k, 1, first:last, :], -1 - p)
        centre = seg(s)
        left = jnp.where(lane == 0, low, turned(centre, 1))
        right = jnp.where(lane == tile - 1, high, turned(centre, -1))
        up = field[p, pl.ds(at[s] - 1, size[s]), :]
        down = field[p, pl.ds(at[s] + 1, size[s]), :]
        kap = kc_ref[...] if s == 1 else kf_ref[:, (s // 2) * tile : (s // 2 + 1) * tile]
        return (4.0 + kap) * centre - (down + up + right + left)

    def own(field, p, s):
        return field[p, pl.ds(at[s], size[s]), :]

    def put(field, p, s, value):
        field[p, pl.ds(at[s], size[s]), :] = value

    input_copy(0).wait()
    input_copy(1).wait()
    fine = (2 * pf_ref[...] - 1).astype(F32)
    z[:, at[0] : at[0] + rows, :] = fine[:, :, :tile]
    z[:, at[2] : at[2] + rows, :] = fine[:, :, tile:]
    z[:, at[1] : at[1] + half_rows, :] = (2 * pc_ref[...] - 1).astype(F32)
    pl.semaphore_wait(barrier, total - 1)
    pack_rows(z, 0)
    row_start(0)
    col_start(z, 0)

    for k in range(2, 6):
        input_copy(k).wait()
    alive = lax.broadcasted_iota(jnp.int32, (blocks, tile), 0) < cnt_ref[0]
    wm[...] = jnp.where(alive, wt_ref[...], 0.0)
    line = lax.broadcasted_iota(jnp.int32, (z.shape[1], blocks), 0)
    per_row = width // tile
    name = jnp.where(
        line <= at[0] + rows,
        per_row * (line - (at[0] - 1)),
        jnp.where(
            line <= at[1] + half_rows,
            (rows + 2) * per_row + line - (at[1] - 1),
            per_row * (line - (at[2] - 1)) + 1,
        ),
    )
    inside = (
        ((line >= at[0] - 1) & (line <= at[0] + rows))
        | ((line >= at[1] - 1) & (line <= at[1] + half_rows))
        | ((line >= at[2] - 1) & (line <= at[2] + rows))
    )
    chosen = jnp.where(inside & (name == idxv_ref[...]), 1.0, 0.0)
    onehot[...] = chosen.astype(BF16)
    pick[...] = chosen.T.astype(BF16)

    def split_chunk(c, _):
        phi_copy(c).wait()
        for k in range(GROUP):
            x = phi32[c * GROUP + k]
            hi = x.astype(BF16)
            ph[c * GROUP + k, 0:tile, :] = hi
            ph[c * GROUP + k, tile : 2 * tile, :] = (x - hi.astype(F32)).astype(BF16)
        return 0

    head = chunks // 2
    lax.fori_loop(0, head, split_chunk, 0)

    def fill_ext(field):
        for p in range(probes):
            x = field[p]
            hi = x.astype(BF16)
            lo = (x - hi.astype(F32)).astype(BF16)
            out = jnp.dot(
                pick[...], jnp.concatenate([hi, lo], axis=1), preferred_element_type=F32
            )
            ext[pl.ds(p, blocks, stride=8), :] = out[:, :tile]
            ext[pl.ds(4 + p, blocks, stride=8), :] = out[:, tile:]

    top = lax.broadcasted_iota(jnp.int32, (8, tile), 0) < 4

    def observe(g, _):
        scaled = []
        for k in range(GROUP):
            b = g * GROUP + k
            got = ext[pl.ds(pl.multiple_of(b * 8, 8), 8), :].astype(BF16)
            seen = lax.dot_general(
                got, ph[b], (((1,), (1,)), ((), ())), preferred_element_type=F32
            )
            seen = seen[:, :tile] + seen[:, tile:]
            seen = seen + pltpu.roll(seen, 4, 0)
            scaled.append(seen * wm[pl.ds(b, 1), :])
        for k in range(GROUP):
            b = g * GROUP + k
            hi = scaled[k].astype(BF16).astype(F32)
            parts = jnp.where(top, hi, scaled[k] - hi).astype(BF16)
            out = lax.dot_general(
                jnp.concatenate([parts, parts], axis=1),
                ph[b],
                (((1,), (0,)), ((), ())),
                preferred_element_type=F32,
            )
            back[pl.ds(pl.multiple_of(b * 8, 8), 8), :] = out + pltpu.roll(out, 4, 0)
        return 0

    def scatter():
        for p in range(probes):
            x = back[pl.ds(p, blocks, stride=8), :]
            hi = x.astype(BF16)
            lo = (x - hi.astype(F32)).astype(BF16)
            out = jnp.dot(
                onehot[...], jnp.concatenate([hi, lo], axis=1), preferred_element_type=F32
            )
            adj[p] = out[:, :tile] + out[:, tile:]

    def ar_copy(k, j):
        return pltpu.make_async_remote_copy(
            src_ref=ar_out.at[k],
            dst_ref=ar_in.at[k, me],
            send_sem=ar_ssem.at[k, j],
            recv_sem=ar_rsem.at[k, me],
            device_id=peer(j),
            device_id_type=MESH,
        )

    def ar_recv(k, j):
        other = lax.rem(me + j, total)
        return pltpu.make_async_remote_copy(
            src_ref=ar_out.at[k],
            dst_ref=ar_in.at[k, other],
            send_sem=ar_ssem.at[k, j],
            recv_sem=ar_rsem.at[k, other],
            device_id=peer(j),
            device_id_type=MESH,
        )

    def ar_start(k):
        for j in range(1, total):
            ar_copy(k, j).start()
        ar_in[k, me] = ar_out[k]

    def ar_wait(k):
        for j in range(1, total):
            ar_recv(k, j).wait_recv()
        acc = ar_in[k, 0]
        for j in range(1, total):
            acc = acc + ar_in[k, j]
        return jnp.sum(acc, axis=1, keepdims=True)

    row_wait(0)
    unpack_rows(z, 0)
    col_wait(0)
    for p in range(probes):
        for s in range(3):
            put(u0, p, s, sar(z, 0, s, p))
    pack_rows(u0, 1)
    row_start(1)
    col_start(u0, 1)
    fill_ext(z)

    def observe_and_split(g, _):
        observe(g, 0)
        return split_chunk(g + head, 0)

    lax.fori_loop(0, chunks - head, observe_and_split, 0)
    lax.fori_loop(chunks - head, chunks, observe, 0)
    scatter()
    row_wait(1)
    unpack_rows(u0, 1)
    col_wait(1)
    for p in range(probes):
        for s in range(3):
            put(q1, p, s, sar(u0, 1, s, p) + own(adj, p, s))
    pack_rows(q1, 2)
    pack_rows(adj, 2, first=4, outside=True)
    row_start(2)
    row_wait(2)
    mask = [jnp.where(h, 1.0, 0.0) for h in has_row]
    for s in range(3):
        edge = (at[s] - 1, at[s] + size[s])
        inner = (at[s], at[s] + size[s] - 1)
        for p in range(probes):
            for d in range(2):
                q1[p, pl.ds(edge[d], 1), :] = (
                    row_in[2, d, s, pl.ds(p, 1), :] + adj[p, pl.ds(edge[d], 1), :] * mask[d]
                )
                q1[p, pl.ds(inner[d], 1), :] = (
                    q1[p, pl.ds(inner[d], 1), :] + row_in[2, d, s, pl.ds(4 + p, 1), :]
                )
    col_start(q1, 2)

    def lanes(first, second, p):
        out = None
        for s in range(3):
            part = jnp.sum(first(p, s) * second(p, s), axis=0, keepdims=True)
            out = part if out is None else out + part
        return out

    own_z = functools.partial(own, z)
    own_q = functools.partial(own, q1)
    for p in range(probes):
        ar_out[0, pl.ds(p, 1), :] = lanes(own_z, own_z, p)
        ar_out[0, pl.ds(4 + p, 1), :] = lanes(own_z, own_q, p)
        ar_out[0, pl.ds(8 + p, 1), :] = lanes(own_q, own_q, p)
    ar_start(0)

    fill_ext(q1)
    lax.fori_loop(0, head, observe, 0)
    col_wait(2)
    for p in range(probes):
        for s in range(3):
            put(u1, p, s, sar(q1, 2, s, p))
    pack_rows(u1, 3)
    row_start(3)
    col_start(u1, 3)
    lax.fori_loop(head, chunks, observe, 0)
    scatter()
    pack_rows(adj, 4, outside=True)
    row_start(4)
    row_wait(3)
    unpack_rows(u1, 3)
    col_wait(3)
    sums = ar_wait(0)
    rr, pq, qq = sums[0:4], sums[4:8], sums[8:12]
    alpha = rr / pq
    grow = alpha * (qq / pq)
    for p in range(probes):
        a1, g1 = alpha[p : p + 1], grow[p : p + 1]
        line_sum, norm_sum = None, None
        for s in range(3):
            image = g1 * own(q1, p, s) - a1 * (sar(u1, 3, s, p) + own(adj, p, s))
            direction = g1 * own(z, p, s) - a1 * own(q1, p, s)
            part = jnp.sum(direction * image, axis=0, keepdims=True)
            for d in range(2):
                edge = (at[s] - 1, at[s] + size[s])[d]
                outside = g1 * z[p, pl.ds(edge, 1), :] - a1 * q1[p, pl.ds(edge, 1), :]
                part = part - a1 * (outside * adj[p, pl.ds(edge, 1), :]) * mask[d]
            line_sum = part if line_sum is None else line_sum + part
            resid = own(z, p, s) - a1 * own(q1, p, s)
            part = jnp.sum(resid * resid, axis=0, keepdims=True)
            norm_sum = part if norm_sum is None else norm_sum + part
            put(im, p, s, image)
        ar_out[1, pl.ds(p, 1), :] = line_sum
        ar_out[1, pl.ds(4 + p, 1), :] = norm_sum
    ar_start(1)

    row_wait(4)
    for s in range(3):
        inner = (at[s], at[s] + size[s] - 1)
        for p in range(probes):
            for d in range(2):
                im[p, pl.ds(inner[d], 1), :] = (
                    im[p, pl.ds(inner[d], 1), :]
                    - alpha[p : p + 1] * row_in[4, d, s, pl.ds(p, 1), :]
                )
    last = ar_wait(1)
    alpha_two = last[4:8] / last[0:4]
    for p in range(probes):
        a1, g1, a2 = alpha[p : p + 1], grow[p : p + 1], alpha_two[p : p + 1]
        for s in range(3):
            zz, qq_ = own(z, p, s), own(q1, p, s)
            solve = a1 * zz + a2 * (g1 * zz - a1 * qq_)
            resid = zz - a1 * qq_ - a2 * own(im, p, s)
            if s == 1:
                xc_ref[p] = solve
                rc_ref[p] = resid
            else:
                columns = slice((s // 2) * tile, (s // 2 + 1) * tile)
                xf_ref[p, :, columns] = solve
                rf_ref[p, :, columns] = resid
    for k in range(5):
        for d in range(2):

            @pl.when(has_row[d])
            def _():
                row_copy(k, d).wait_send()

    for k in range(4):
        for d in range(2):

            @pl.when(has_col[d])
            def _():
                col_copy(k, d).wait_send()

    for k in range(2):
        for j in range(1, total):
            ar_copy(k, j).wait_send()


def write_out(*refs):
    sources, targets, sem = refs[:4], refs[4:8], refs[8]
    copies = [pltpu.make_async_copy(sources[k], targets[k], sem.at[k]) for k in range(4)]
    for copy in copies:
        copy.start()
    for copy in copies:
        copy.wait()


def local(
    n_ew,
    n_ns,
    probe_fine,
    probe_coarse,
    kappa_fine,
    kappa_coarse,
    phi_tiles,
    obs_weight,
    block_index,
    block_count,
):
    probes, rows, width = probe_fine.shape
    half_rows, tile = probe_coarse.shape[1:]
    blocks = phi_tiles.shape[0]
    lines = 2 * rows + half_rows + 48
    total = n_ew * n_ns
    vmem = pl.BlockSpec(memory_space=pltpu.VMEM)
    smem = pl.BlockSpec(memory_space=pltpu.SMEM)
    field = pltpu.VMEM((probes, lines, tile), F32)
    dma = pltpu.SemaphoreType.DMA
    results = pl.pallas_call(
        functools.partial(kernel, n_ew, n_ns),
        out_shape=(
            jax.ShapeDtypeStruct(probe_fine.shape, F32),
            jax.ShapeDtypeStruct(probe_coarse.shape, F32),
            jax.ShapeDtypeStruct(probe_fine.shape, F32),
            jax.ShapeDtypeStruct(probe_coarse.shape, F32),
        ),
        in_specs=[pl.BlockSpec(memory_space=pltpu.HBM)] * 7 + [smem],
        out_specs=(vmem,) * 4,
        scratch_shapes=[
            pltpu.VMEM(probe_fine.shape, jnp.int32),
            pltpu.VMEM(probe_coarse.shape, jnp.int32),
            pltpu.VMEM(kappa_fine.shape, F32),
            pltpu.VMEM(kappa_coarse.shape, F32),
            pltpu.VMEM(obs_weight.shape, F32),
            pltpu.VMEM((1, blocks), jnp.int32),
            pltpu.VMEM(phi_tiles.shape, F32),
            pltpu.VMEM((blocks, 2 * tile, tile), BF16),
            field,
            field,
            field,
            field,
            field,
            field,
            pltpu.VMEM((blocks * 8, tile), F32),
            pltpu.VMEM((blocks * 8, tile), F32),
            pltpu.VMEM((blocks, tile), F32),
            pltpu.VMEM((lines, blocks), BF16),
            pltpu.VMEM((blocks, lines), BF16),
            pltpu.VMEM((5, 2, 3, 8, tile), F32),
            pltpu.VMEM((5, 2, 3, 8, tile), F32),
            pltpu.VMEM((4, 2, rows + half_rows, tile), F32),
            pltpu.VMEM((4, 2, rows + half_rows, tile), F32),
            pltpu.VMEM((2, 16, tile), F32),
            pltpu.VMEM((2, total, 16, tile), F32),
            dma((6,)),
            dma((blocks // GROUP,)),
            dma((5, 2)),
            dma((5, 2)),
            dma((4, 2)),
            dma((4, 2)),
            dma((2, total)),
            dma((2, total)),
        ],
        compiler_params=pltpu.CompilerParams(
            collective_id=0, has_side_effects=True, vmem_limit_bytes=VMEM_BYTES
        ),
        cost_estimate=pl.CostEstimate(
            flops=4 * blocks * tile * tile * 8 * 4, bytes_accessed=phi_tiles.size * 4, transcendentals=0
        ),
    )(
        probe_fine,
        probe_coarse,
        kappa_fine,
        kappa_coarse,
        phi_tiles,
        obs_weight,
        block_index.reshape(1, blocks),
        block_count,
    )
    return pl.pallas_call(
        write_out,
        out_shape=tuple(jax.ShapeDtypeStruct(r.shape, F32) for r in results),
        in_specs=[vmem] * 4,
        out_specs=(pl.BlockSpec(memory_space=pltpu.HBM),) * 4,
        scratch_shapes=[dma((4,))],
    )(*results)


def solution(mesh):
    in_specs = (
        P("lvl", "ew", "ns"),
        P("lvl", "ew", "ns"),
        P(("grp", "ew"), "ns"),
        P(("grp", "ew"), "ns"),
        P(("ew", "ns"), None, None),
        P(("grp", "ew", "ns"), None),
        P(("ew", "ns")),
        P(("ew", "ns")),
    )
    out_specs = (P(("grp", "lvl"), "ew", "ns"),) * 4
    body = functools.partial(local, mesh.shape["ew"], mesh.shape["ns"])
    return jax.shard_map(body, mesh=mesh, in_specs=in_specs, out_specs=out_specs, check_vma=False)
```

```python
import functools

import jax
import jax.numpy as jnp
from jax import lax
from jax.experimental import pallas as pl
from jax.experimental.pallas import tpu as pltpu
from jax.sharding import PartitionSpec as P

MESH = pl.DeviceIdType.MESH
GROUP = 32
VMEM_BYTES = 64 * 2**20 - 2**16
F32 = jnp.float32
BF16 = jnp.bfloat16


def kernel(
    n_ew,
    n_ns,
    pf_hbm,
    pc_hbm,
    kf_hbm,
    kc_hbm,
    phi_ref,
    wt_hbm,
    idxv_hbm,
    cnt_ref,
    xf_ref,
    xc_ref,
    rf_ref,
    rc_ref,
    pf_ref,
    pc_ref,
    kf_ref,
    kc_ref,
    wt_ref,
    idxv_ref,
    phi32,
    ph,
    z,
    u0,
    q1,
    u1,
    adj,
    im,
    ext,
    back,
    wm,
    onehot,
    pick,
    row_out,
    row_in,
    col_out,
    col_in,
    ar_out,
    ar_in,
    in_sem,
    phi_sem,
    row_ssem,
    row_rsem,
    col_ssem,
    col_rsem,
    ar_ssem,
    ar_rsem,
):
    probes, rows, width = pf_ref.shape
    half_rows = pc_ref.shape[1]
    tile = pc_ref.shape[2]
    blocks = ph.shape[0]
    at = (8, rows + 24, rows + half_rows + 40)
    size = (rows, half_rows, rows)
    chunks = blocks // GROUP
    total = n_ew * n_ns
    e = lax.axis_index("ew")
    n = lax.axis_index("ns")
    me = e * n_ns + n
    has_row = (e > 0, e < n_ew - 1)
    has_col = (n > 0, n < n_ns - 1)
    row_dev = ({"ew": lax.max(e - 1, 0)}, {"ew": lax.min(e + 1, n_ew - 1)})
    col_dev = ({"ns": lax.max(n - 1, 0)}, {"ns": lax.min(n + 1, n_ns - 1)})

    def input_copy(k):
        source, target = (
            (pf_hbm, pf_ref),
            (pc_hbm, pc_ref),
            (wt_hbm, wt_ref),
            (idxv_hbm, idxv_ref),
            (kf_hbm, kf_ref),
            (kc_hbm, kc_ref),
        )[k]
        return pltpu.make_async_copy(source, target, in_sem.at[k])

    for k in range(6):
        input_copy(k).start()

    def phi_copy(c):
        part = pl.ds(c * GROUP, GROUP)
        return pltpu.make_async_copy(phi_ref.at[part], phi32.at[part], phi_sem.at[c]
        )

    def start_phi(c, _):
        phi_copy(c).start()
        return 0

    lax.fori_loop(0, chunks, start_phi, 0)

    def peer(k):
        other = lax.rem(me + k, total)
        return {"ew": other // n_ns, "ns": lax.rem(other, n_ns)}

    barrier = pltpu.get_barrier_semaphore()
    for k in range(1, total):
        pl.semaphore_signal(barrier, inc=1, device_id=peer(k), device_id_type=MESH)

    z[...] = jnp.zeros_like(z)
    u0[...] = jnp.zeros_like(u0)
    q1[...] = jnp.zeros_like(q1)
    u1[...] = jnp.zeros_like(u1)
    row_out[...] = jnp.zeros_like(row_out)
    ar_out[...] = jnp.zeros_like(ar_out)
    for d in range(2):

        @pl.when(jnp.logical_not(has_row[d]))
        def _():
            for k in range(5):
                row_in[k, d] = jnp.zeros(row_in.shape[2:], F32)

        @pl.when(jnp.logical_not(has_col[d]))
        def _():
            for k in range(4):
                col_in[k, d] = jnp.zeros(col_in.shape[2:], F32)

    def row_copy(k, d):
        return pltpu.make_async_remote_copy(
            src_ref=row_out.at[k, d],
            dst_ref=row_in.at[k, 1 - d],
            send_sem=row_ssem.at[k, d],
            recv_sem=row_rsem.at[k, 1 - d],
            device_id=row_dev[d],
            device_id_type=MESH,
        )

    def row_start(k):
        for d in range(2):

            @pl.when(has_row[d])
            def _():
                row_copy(k, d).start()

    def row_wait(k):
        for d in range(2):

            @pl.when(has_row[d])
            def _():
                row_copy(k, 1 - d).wait_recv()

    def turned(x, distance):
        return pltpu.roll(x, distance % tile, 1) if distance % tile else x

    def pack_cols(field, k):
        for d in range(2):
            edge = (0, tile - 1)[d]
            for s, first in ((2 * d, 0), (1, rows)):
                lane = lax.broadcasted_iota(jnp.int32, (size[s], tile), 1)
                packed = jnp.zeros((size[s], tile), F32)
                for p in range(probes):
                    moved = turned(field[p, pl.ds(at[s], size[s]), :], p - edge)
                    packed = jnp.where(lane == p, moved, packed)
                col_out[k, d, pl.ds(first, size[s]), :] = packed

    def col_copy(k, d):
        return pltpu.make_async_remote_copy(
            src_ref=col_out.at[k, d],
            dst_ref=col_in.at[k, 1 - d],
            send_sem=col_ssem.at[k, d],
            recv_sem=col_rsem.at[k, 1 - d],
            device_id=col_dev[d],
            device_id_type=MESH,
        )

    def col_start(field, k):
        pack_cols(field, k)
        for d in range(2):

            @pl.when(has_col[d])
            def _():
                col_copy(k, d).start()

    def col_wait(k):
        for d in range(2):

            @pl.when(has_col[d])
            def _():
                col_copy(k, 1 - d).wait_recv()

    def pack_rows(field, k, first=0, outside=False):
        for s in range(3):
            low, high = at[s], at[s] + size[s] - 1
            if outside:
                low, high = low - 1, high + 1
            for p in range(probes):
                row_out[k, 0, s, pl.ds(first + p, 1), :] = field[p, pl.ds(low, 1), :]
                row_out[k, 1, s, pl.ds(first + p, 1), :] = field[p, pl.ds(high, 1), :]

    def unpack_rows(field, k):
        for s in range(3):
            for p in range(probes):
                field[p, pl.ds(at[s] - 1, 1), :] = row_in[k, 0, s, pl.ds(p, 1), :]
                field[p, pl.ds(at[s] + size[s], 1), :] = row_in[k, 1, s, pl.ds(p, 1), :]

    def sar(field, k, s, p):
        lane = lax.broadcasted_iota(jnp.int32, (size[s], tile), 1)

        def seg(which):
            return field[p, pl.ds(at[which], size[which]), :]

        first, last = (0, rows) if s != 1 else (rows, rows + half_rows)
        low = turned(seg(0), 1) if s == 2 else turned(col_in[k, 0, first:last, :], -p)
        high = turned(seg(2), -1) if s == 0 else turned(col_in[k, 1, first:last, :], -1 - p)
        centre = seg(s)
        left = jnp.where(lane == 0, low, turned(centre, 1))
        right = jnp.where(lane == tile - 1, high, turned(centre, -1))
        up = field[p, pl.ds(at[s] - 1, size[s]), :]
        down = field[p, pl.ds(at[s] + 1, size[s]), :]
        kap = kc_ref[...] if s == 1 else kf_ref[:, (s // 2) * tile : (s // 2 + 1) * tile]
        return (4.0 + kap) * centre - (down + up + right + left)

    def own(field, p, s):
        return field[p, pl.ds(at[s], size[s]), :]

    def put(field, p, s, value):
        field[p, pl.ds(at[s], size[s]), :] = value

    input_copy(0).wait()
    input_copy(1).wait()
    fine = (2 * pf_ref[...] - 1).astype(F32)
    z[:, at[0] : at[0] + rows, :] = fine[:, :, :tile]
    z[:, at[2] : at[2] + rows, :] = fine[:, :, tile:]
    z[:, at[1] : at[1] + half_rows, :] = (2 * pc_ref[...] - 1).astype(F32)
    pl.semaphore_wait(barrier, total - 1)
    pack_rows(z, 0)
    row_start(0)
    col_start(z, 0)

    for k in range(2, 6):
        input_copy(k).wait()
    alive = lax.broadcasted_iota(jnp.int32, (blocks, tile), 0) < cnt_ref[0]
    wm[...] = jnp.where(alive, wt_ref[...], 0.0)
    line = lax.broadcasted_iota(jnp.int32, (z.shape[1], blocks), 0)
    per_row = width // tile
    name = jnp.where(
        line <= at[0] + rows,
        per_row * (line - (at[0] - 1)),
        jnp.where(
            line <= at[1] + half_rows,
            (rows + 2) * per_row + line - (at[1] - 1),
            per_row * (line - (at[2] - 1)) + 1,
        ),
    )
    inside = (
        ((line >= at[0] - 1) & (line <= at[0] + rows))
        | ((line >= at[1] - 1) & (line <= at[1] + half_rows))
        | ((line >= at[2] - 1) & (line <= at[2] + rows))
    )
    chosen = jnp.where(inside & (name == idxv_ref[...]), 1.0, 0.0)
    onehot[...] = chosen.astype(BF16)
    pick[...] = chosen.T.astype(BF16)

    def split_chunk(c, _):
        phi_copy(c).wait()
        for k in range(GROUP):
            x = phi32[c * GROUP + k]
            hi = x.astype(BF16)
            ph[c * GROUP + k, 0:tile, :] = hi
            ph[c * GROUP + k, tile : 2 * tile, :] = (x - hi.astype(F32)).astype(BF16)
        return 0

    head = chunks // 2
    lax.fori_loop(0, head, split_chunk, 0)

    def fill_ext(field):
        for p in range(probes):
            x = field[p]
            hi = x.astype(BF16)
            lo = (x - hi.astype(F32)).astype(BF16)
            out = jnp.dot(
                pick[...], jnp.concatenate([hi, lo], axis=1), preferred_element_type=F32
            )
            ext[pl.ds(p, blocks, stride=8), :] = out[:, :tile]
            ext[pl.ds(4 + p, blocks, stride=8), :] = out[:, tile:]

    top = lax.broadcasted_iota(jnp.int32, (8, tile), 0) < 4

    def observe(g, _):
        scaled = []
        for k in range(GROUP):
            b = g * GROUP + k
            got = ext[pl.ds(pl.multiple_of(b * 8, 8), 8), :].astype(BF16)
            seen = lax.dot_general(
                got, ph[b], (((1,), (1,)), ((), ())), preferred_element_type=F32
            )
            seen = seen[:, :tile] + seen[:, tile:]
            seen = seen + pltpu.roll(seen, 4, 0)
            scaled.append(seen * wm[pl.ds(b, 1), :])
        for k in range(GROUP):
            b = g * GROUP + k
            hi = scaled[k].astype(BF16).astype(F32)
            parts = jnp.where(top, hi, scaled[k] - hi).astype(BF16)
            out = lax.dot_general(
                jnp.concatenate([parts, parts], axis=1),
                ph[b],
                (((1,), (0,)), ((), ())),
                preferred_element_type=F32,
            )
            back[pl.ds(pl.multiple_of(b * 8, 8), 8), :] = out + pltpu.roll(out, 4, 0)
        return 0

    def scatter():
        for p in range(probes):
            x = back[pl.ds(p, blocks, stride=8), :]
            hi = x.astype(BF16)
            lo = (x - hi.astype(F32)).astype(BF16)
            out = jnp.dot(
                onehot[...], jnp.concatenate([hi, lo], axis=1), preferred_element_type=F32
            )
            adj[p] = out[:, :tile] + out[:, tile:]

    def ar_copy(k, j):
        return pltpu.make_async_remote_copy(
            src_ref=ar_out.at[k],
            dst_ref=ar_in.at[k, me],
            send_sem=ar_ssem.at[k, j],
            recv_sem=ar_rsem.at[k, me],
            device_id=peer(j),
            device_id_type=MESH,
        )

    def ar_recv(k, j):
        other = lax.rem(me + j, total)
        return pltpu.make_async_remote_copy(
            src_ref=ar_out.at[k],
            dst_ref=ar_in.at[k, other],
            send_sem=ar_ssem.at[k, j],
            recv_sem=ar_rsem.at[k, other],
            device_id=peer(j),
            device_id_type=MESH,
        )

    def ar_start(k):
        for j in range(1, total):
            ar_copy(k, j).start()
        ar_in[k, me] = ar_out[k]

    def ar_wait(k):
        for j in range(1, total):
            ar_recv(k, j).wait_recv()
        acc = ar_in[k, 0]
        for j in range(1, total):
            acc = acc + ar_in[k, j]
        return jnp.sum(acc, axis=1, keepdims=True)

    row_wait(0)
    unpack_rows(z, 0)
    col_wait(0)
    for p in range(probes):
        for s in range(3):
            put(u0, p, s, sar(z, 0, s, p))
    pack_rows(u0, 1)
    row_start(1)
    col_start(u0, 1)
    fill_ext(z)

    def observe_and_split(g, _):
        observe(g, 0)
        return split_chunk(g + head, 0)

    lax.fori_loop(0, chunks - head, observe_and_split, 0)
    lax.fori_loop(chunks - head, chunks, observe, 0)
    scatter()
    row_wait(1)
    unpack_rows(u0, 1)
    col_wait(1)
    for p in range(probes):
        for s in range(3):
            put(q1, p, s, sar(u0, 1, s, p) + own(adj, p, s))
    pack_rows(q1, 2)
    pack_rows(adj, 2, first=4, outside=True)
    row_start(2)
    row_wait(2)
    mask = [jnp.where(h, 1.0, 0.0) for h in has_row]
    for s in range(3):
        edge = (at[s] - 1, at[s] + size[s])
        inner = (at[s], at[s] + size[s] - 1)
        for p in range(probes):
            for d in range(2):
                q1[p, pl.ds(edge[d], 1), :] = (
                    row_in[2, d, s, pl.ds(p, 1), :] + adj[p, pl.ds(edge[d], 1), :] * mask[d]
                )
                q1[p, pl.ds(inner[d], 1), :] = (
                    q1[p, pl.ds(inner[d], 1), :] + row_in[2, d, s, pl.ds(4 + p, 1), :]
                )
    col_start(q1, 2)

    def lanes(first, second, p):
        out = None
        for s in range(3):
            part = jnp.sum(first(p, s) * second(p, s), axis=0, keepdims=True)
            out = part if out is None else out + part
        return out

    own_z = functools.partial(own, z)
    own_q = functools.partial(own, q1)
    for p in range(probes):
        ar_out[0, pl.ds(p, 1), :] = lanes(own_z, own_z, p)
        ar_out[0, pl.ds(4 + p, 1), :] = lanes(own_z, own_q, p)
        ar_out[0, pl.ds(8 + p, 1), :] = lanes(own_q, own_q, p)
    ar_start(0)

    fill_ext(q1)
    lax.fori_loop(0, head, observe, 0)
    col_wait(2)
    for p in range(probes):
        for s in range(3):
            put(u1, p, s, sar(q1, 2, s, p))
    pack_rows(u1, 3)
    row_start(3)
    col_start(u1, 3)
    lax.fori_loop(head, chunks, observe, 0)
    scatter()
    pack_rows(adj, 4, outside=True)
    row_start(4)
    row_wait(3)
    unpack_rows(u1, 3)
    col_wait(3)
    sums = ar_wait(0)
    rr, pq, qq = sums[0:4], sums[4:8], sums[8:12]
    alpha = rr / pq
    grow = alpha * (qq / pq)
    for p in range(probes):
        a1, g1 = alpha[p : p + 1], grow[p : p + 1]
        line_sum, norm_sum = None, None
        for s in range(3):
            image = g1 * own(q1, p, s) - a1 * (sar(u1, 3, s, p) + own(adj, p, s))
            direction = g1 * own(z, p, s) - a1 * own(q1, p, s)
            part = jnp.sum(direction * image, axis=0, keepdims=True)
            for d in range(2):
                edge = (at[s] - 1, at[s] + size[s])[d]
                outside = g1 * z[p, pl.ds(edge, 1), :] - a1 * q1[p, pl.ds(edge, 1), :]
                part = part - a1 * (outside * adj[p, pl.ds(edge, 1), :]) * mask[d]
            line_sum = part if line_sum is None else line_sum + part
            resid = own(z, p, s) - a1 * own(q1, p, s)
            part = jnp.sum(resid * resid, axis=0, keepdims=True)
            norm_sum = part if norm_sum is None else norm_sum + part
            put(im, p, s, image)
        ar_out[1, pl.ds(p, 1), :] = line_sum
        ar_out[1, pl.ds(4 + p, 1), :] = norm_sum
    ar_start(1)

    row_wait(4)
    for s in range(3):
        inner = (at[s], at[s] + size[s] - 1)
        for p in range(probes):
            for d in range(2):
                im[p, pl.ds(inner[d], 1), :] = (
                    im[p, pl.ds(inner[d], 1), :]
                    - alpha[p : p + 1] * row_in[4, d, s, pl.ds(p, 1), :]
                )
    last = ar_wait(1)
    alpha_two = last[4:8] / last[0:4]
    for p in range(probes):
        a1, g1, a2 = alpha[p : p + 1], grow[p : p + 1], alpha_two[p : p + 1]
        for s in range(3):
            zz, qq_ = own(z, p, s), own(q1, p, s)
            solve = a1 * zz + a2 * (g1 * zz - a1 * qq_)
            resid = zz - a1 * qq_ - a2 * own(im, p, s)
            if s == 1:
                xc_ref[p] = solve
                rc_ref[p] = resid
            else:
                columns = slice((s // 2) * tile, (s // 2 + 1) * tile)
                xf_ref[p, :, columns] = solve
                rf_ref[p, :, columns] = resid
    for k in range(5):
        for d in range(2):

            @pl.when(has_row[d])
            def _():
                row_copy(k, d).wait_send()

    for k in range(4):
        for d in range(2):

            @pl.when(has_col[d])
            def _():
                col_copy(k, d).wait_send()

    for k in range(2):
        for j in range(1, total):
            ar_copy(k, j).wait_send()


def write_out(*refs):
    sources, targets, held, sem = refs[:4], refs[4:8], refs[8:12], refs[12]
    reads = [pltpu.make_async_copy(sources[k], held[k], sem.at[0, k]) for k in range(4)]
    writes = [pltpu.make_async_copy(held[k], targets[k], sem.at[1, k]) for k in range(4)]
    for copy in reads:
        copy.start()
    for k in range(4):
        reads[k].wait()
        writes[k].start()
    for copy in writes:
        copy.wait()


def local(
    n_ew,
    n_ns,
    probe_fine,
    probe_coarse,
    kappa_fine,
    kappa_coarse,
    phi_tiles,
    obs_weight,
    block_index,
    block_count,
):
    probes, rows, width = probe_fine.shape
    half_rows, tile = probe_coarse.shape[1:]
    blocks = phi_tiles.shape[0]
    lines = 2 * rows + half_rows + 48
    total = n_ew * n_ns
    vmem = pl.BlockSpec(memory_space=pltpu.VMEM)
    smem = pl.BlockSpec(memory_space=pltpu.SMEM)
    field = pltpu.VMEM((probes, lines, tile), F32)
    dma = pltpu.SemaphoreType.DMA
    results = pl.pallas_call(
        functools.partial(kernel, n_ew, n_ns),
        out_shape=(
            jax.ShapeDtypeStruct(probe_fine.shape, F32),
            jax.ShapeDtypeStruct(probe_coarse.shape, F32),
            jax.ShapeDtypeStruct(probe_fine.shape, F32),
            jax.ShapeDtypeStruct(probe_coarse.shape, F32),
        ),
        in_specs=[pl.BlockSpec(memory_space=pltpu.HBM)] * 7 + [smem],
        out_specs=(vmem,) * 4,
        scratch_shapes=[
            pltpu.VMEM(probe_fine.shape, jnp.int32),
            pltpu.VMEM(probe_coarse.shape, jnp.int32),
            pltpu.VMEM(kappa_fine.shape, F32),
            pltpu.VMEM(kappa_coarse.shape, F32),
            pltpu.VMEM(obs_weight.shape, F32),
            pltpu.VMEM((1, blocks), jnp.int32),
            pltpu.VMEM(phi_tiles.shape, F32),
            pltpu.VMEM((blocks, 2 * tile, tile), BF16),
            field,
            field,
            field,
            field,
            field,
            field,
            pltpu.VMEM((blocks * 8, tile), F32),
            pltpu.VMEM((blocks * 8, tile), F32),
            pltpu.VMEM((blocks, tile), F32),
            pltpu.VMEM((lines, blocks), BF16),
            pltpu.VMEM((blocks, lines), BF16),
            pltpu.VMEM((5, 2, 3, 8, tile), F32),
            pltpu.VMEM((5, 2, 3, 8, tile), F32),
            pltpu.VMEM((4, 2, rows + half_rows, tile), F32),
            pltpu.VMEM((4, 2, rows + half_rows, tile), F32),
            pltpu.VMEM((2, 16, tile), F32),
            pltpu.VMEM((2, total, 16, tile), F32),
            dma((6,)),
            dma((blocks // GROUP,)),
            dma((5, 2)),
            dma((5, 2)),
            dma((4, 2)),
            dma((4, 2)),
            dma((2, total)),
            dma((2, total)),
        ],
        compiler_params=pltpu.CompilerParams(
            collective_id=0, has_side_effects=True, vmem_limit_bytes=VMEM_BYTES
        ),
        cost_estimate=pl.CostEstimate(
            flops=4 * blocks * tile * tile * 8 * 4, bytes_accessed=phi_tiles.size * 4, transcendentals=0
        ),
    )(
        probe_fine,
        probe_coarse,
        kappa_fine,
        kappa_coarse,
        phi_tiles,
        obs_weight,
        block_index.reshape(1, blocks),
        block_count,
    )
    return pl.pallas_call(
        write_out,
        out_shape=tuple(jax.ShapeDtypeStruct(r.shape, F32) for r in results),
        in_specs=[pl.BlockSpec(memory_space=pltpu.HBM)] * 4,
        out_specs=(pl.BlockSpec(memory_space=pltpu.HBM),) * 4,
        scratch_shapes=[pltpu.VMEM(r.shape, F32) for r in results] + [dma((2, 4))],
        compiler_params=pltpu.CompilerParams(vmem_limit_bytes=VMEM_BYTES),
    )(*results)


def solution(mesh):
    in_specs = (
        P("lvl", "ew", "ns"),
        P("lvl", "ew", "ns"),
        P(("grp", "ew"), "ns"),
        P(("grp", "ew"), "ns"),
        P(("ew", "ns"), None, None),
        P(("grp", "ew", "ns"), None),
        P(("ew", "ns")),
        P(("ew", "ns")),
    )
    out_specs = (P(("grp", "lvl"), "ew", "ns"),) * 4
    body = functools.partial(local, mesh.shape["ew"], mesh.shape["ns"])
    return jax.shard_map(body, mesh=mesh, in_specs=in_specs, out_specs=out_specs, check_vma=False)
```
